32 devices in a mesh: groups: 2 (over y), ctx: 4 (over z), head: 2 (over x), rep: 2 (over core).
Axes of the slice: x: 2, y: 2, z: 4, core: 2. Of those that a mesh axis runs over, the one named last changes fastest.
Arguments:
- queries: bfloat16 [4096, 4096], P(('groups', 'ctx', 'rep'), 'head'), parts along dimension 0, may hold values from -20 to 20
- keys: bfloat16 [4096, 512], P(('groups', 'ctx', 'rep'), 'head'), parts along dimension 0, may hold values from -20 to 20
- values: bfloat16 [4096, 512], P(('groups', 'ctx', 'rep'), 'head'), parts along dimension 0, may hold values from -6 to 6
- span_order: int32 [16], P('groups'), parts along dimension 0, may hold values from 0 to 7, each once
Outputs:
- attended: bfloat16 [4096, 4096], P(('groups', 'ctx', 'rep'), 'head'), parts along dimension 0
- heavy: float32 [8, 2048], P(('groups', 'head'), ('ctx', 'rep')), parts along dimension 0
The draws below stay inside these ranges and needn't reach their ends.
There are 2 independent parts, one for each index of `groups`. The reference program is written for one: setup_inputs(seed, part) draws one part's arguments, and reference() takes and returns one part's arrays. A program takes and returns all parts, laid end to end along the dimension named above; each array names one. Nothing has to cross between parts.
Inputs may be any that keep to these rules, and one draw needn't show every extreme that they name: `span_order`: every sub-block of 256 positions stands in exactly one slot.
All inputs are finite; a program needn't handle non-finite values.
Results may differ from the reference program's by a relative error of at most 0.0045.
Values may be sent and summed in bfloat16 or wider, within the bound.
A program may use at most 64 MiB of HBM per device.

```python
import jax
import jax.numpy as jnp
from jax import lax

QUERY_HEADS = 32
KEY_VALUE_HEADS = 4
HEAD_WIDTH = 128
SUB = 256
PROMPT_TOKENS = 2048
NSUB = 8


def draw_keys(key, part):
    key = jax.random.fold_in(key, 5)
    offset_start = jax.random.truncated_normal(jax.random.fold_in(key, 1), -4.0, 4.0, (PROMPT_TOKENS, KEY_VALUE_HEADS, HEAD_WIDTH))
    final_output = offset_start
    return final_output.reshape(PROMPT_TOKENS, KEY_VALUE_HEADS * HEAD_WIDTH).astype(jnp.bfloat16)


def draw_queries(key, part):
    key = jax.random.fold_in(key, 7)
    group_width = QUERY_HEADS // KEY_VALUE_HEADS
    offset_start = jax.random.truncated_normal(jax.random.fold_in(key, 1), -4.0, 4.0, (PROMPT_TOKENS, KEY_VALUE_HEADS, group_width, HEAD_WIDTH))
    final_output = offset_start
    return final_output.reshape(PROMPT_TOKENS, QUERY_HEADS * HEAD_WIDTH).astype(jnp.bfloat16)


def shard_levels(own_key, dims, shards, low, high):
    gain, own = 1.0, jax.random.fold_in(own_key, 6)
    for dim, blocks in shards:
        steps = jnp.exp(jax.random.uniform(jax.random.fold_in(own, dim), (blocks,), jnp.float32, low / len(shards), high / len(shards)))
        gain = gain * jnp.repeat(steps, dims[dim] // blocks).reshape([-1 if axis == dim else 1 for axis in range(len(dims))])
    return gain


def bell_draw(own_key, extent, scale, bound, split=(), kind=jnp.bfloat16):
    level = shard_levels(own_key, extent, split, -0.22, 0.18) if split else 1.0
    entries = jax.random.normal(own_key, extent, jnp.float32) * scale * level
    return jnp.minimum(jnp.maximum(entries, -bound), bound).astype(kind)


def setup_inputs(seed: int = 0, part: int = 0) -> dict:
    key_of = jax.random.split(jax.random.key(seed), 5)
    own_keys = jax.random.split(jax.random.fold_in(key_of[4], part), 5)
    return {
        "queries": draw_queries(jax.random.fold_in(jax.random.fold_in(key_of[4], part), 71), part),
        "keys": draw_keys(jax.random.fold_in(jax.random.fold_in(key_of[4], part), 71), part),
        "values": bell_draw(own_keys[2], (PROMPT_TOKENS, KEY_VALUE_HEADS * HEAD_WIDTH), 1.0, 6.0, ((0, 8), (1, 2))),
        "span_order": jax.random.permutation(own_keys[3], NSUB).astype(jnp.int32),
    }


NEG = -1.0e30


def reference(queries, keys, values, span_order):
    group_width = QUERY_HEADS // KEY_VALUE_HEADS
    position = (span_order[:, None] * SUB + jnp.arange(SUB, dtype=jnp.int32)[None, :]).reshape(PROMPT_TOKENS).astype(jnp.int32)
    query_head_rows = queries.reshape(PROMPT_TOKENS, KEY_VALUE_HEADS, group_width, HEAD_WIDTH)
    key_head_rows = keys.reshape(PROMPT_TOKENS, KEY_VALUE_HEADS, HEAD_WIDTH)
    value_head_rows = values.reshape(PROMPT_TOKENS, KEY_VALUE_HEADS, HEAD_WIDTH)
    tile_block = min(512, PROMPT_TOKENS)
    score_scale = HEAD_WIDTH ** -0.5

    def single_block(hitter_score_sum, index):
        start = (index * tile_block).astype(jnp.int32)
        query_block = lax.dynamic_slice_in_dim(query_head_rows, start, tile_block, 0)
        query_pos = lax.dynamic_slice_in_dim(position, start, tile_block, 0)

        def head_results(kv_index):
            query_mat = query_block[:, kv_index].astype(jnp.float32)
            key_mat = key_head_rows[:, kv_index].astype(jnp.float32)
            value_mat = value_head_rows[:, kv_index].astype(jnp.float32)
            scores = jnp.einsum("qgd,kd->gqk", query_mat, key_mat) * score_scale
            allowed = position[None, None, :] <= query_pos[None, :, None]
            scores = jnp.where(allowed, scores, NEG)
            rowmax = jnp.max(scores, axis=-1)
            expo = jnp.where(allowed, jnp.exp(scores - rowmax[..., None]), 0.0)
            rowsum = jnp.sum(expo, axis=-1)
            weights = expo.astype(jnp.bfloat16)
            output = jnp.einsum("gqk,kd->gqd", weights.astype(jnp.float32), value_mat)
            output = (output / rowsum[..., None]).astype(jnp.bfloat16)
            column = jnp.sum(expo / rowsum[..., None], axis=(0, 1))
            return output, column

        output_list, column_span = lax.map(head_results, jnp.arange(KEY_VALUE_HEADS, dtype=jnp.int32))
        output_list = output_list.transpose(2, 0, 1, 3).reshape(tile_block, QUERY_HEADS * HEAD_WIDTH)
        return hitter_score_sum + column_span, output_list

    hitter_score_sum, block_list = lax.scan(single_block, jnp.zeros((KEY_VALUE_HEADS, PROMPT_TOKENS), jnp.float32), jnp.arange(PROMPT_TOKENS // tile_block, dtype=jnp.int32))
    attended = block_list.reshape(PROMPT_TOKENS, QUERY_HEADS * HEAD_WIDTH)
    return attended, hitter_score_sum / group_width
```

```python
import functools
import math

import jax
import jax.numpy as jnp
from jax import lax
from jax.experimental import pallas as pl
from jax.experimental.pallas import tpu as pltpu
from jax.sharding import PartitionSpec as P

HEAD_WIDTH = 128
SPLIT = 1


NEG = -1e30


def positions(order_table, first_row, count, sub_rows):
    row_index = first_row + jnp.arange(count, dtype=jnp.int32)
    return jnp.take(order_table, row_index // sub_rows) * sub_rows + row_index % sub_rows


def absorb(carried, key_block, value_block, key_pos, query_part, pos_part, score_scale):
    maxima, totals, sums = carried
    scores = (
        jnp.einsum("qhgd,khd->hgqk", query_part, key_block, preferred_element_type=jnp.float32)
        * score_scale
    )
    allowed = key_pos[None, None, None, :] <= pos_part[None, None, :, None]
    scores = jnp.where(allowed, scores, NEG)
    fresh = jnp.maximum(maxima, jnp.max(scores, axis=-1))
    expo = jnp.where(allowed, jnp.exp(scores - fresh[..., None]), 0.0)
    factor = jnp.exp(maxima - fresh)
    totals = totals * factor + jnp.sum(expo, axis=-1)
    weights = expo.astype(jnp.bfloat16)
    sums = sums * factor[..., None] + jnp.einsum(
        "hgqk,khd->hgqd", weights, value_block, preferred_element_type=jnp.float32
    )
    return (fresh, totals, sums)


def on_device(queries, keys, values, span_order):
    row_count = queries.shape[0]
    kv_heads = keys.shape[1] // HEAD_WIDTH
    group_width = queries.shape[1] // keys.shape[1]
    sub_rows = row_count // SPLIT
    score_scale = HEAD_WIDTH ** (-0.5)
    device_rank = lax.axis_index(("ctx", "rep"))
    query_pos = positions(span_order, device_rank * row_count, row_count, sub_rows)
    query_mat = queries.reshape(row_count, kv_heads, group_width, HEAD_WIDTH)

    def visit(carried, key_block, value_block, key_pos):
        needed = jnp.min(key_pos) <= jnp.max(query_pos)
        return lax.cond(
            needed,
            lambda inner: absorb(
                inner, key_block, value_block, key_pos, query_mat, query_pos, score_scale
            ),
            lambda inner: inner,
            carried,
        )

    initial = (
        jnp.full((kv_heads, group_width, row_count), NEG, jnp.float32),
        jnp.zeros((kv_heads, group_width, row_count), jnp.float32),
        jnp.zeros((kv_heads, group_width, row_count, HEAD_WIDTH), jnp.float32),
    )
    carried = initial
    key_piece = lax.all_gather(keys, ("ctx", "rep"), axis=0, tiled=True)
    value_piece = lax.all_gather(values, ("ctx", "rep"), axis=0, tiled=True)
    length = key_piece.shape[0]
    count = length // row_count
    key_blocks = key_piece.reshape(count, row_count, kv_heads, HEAD_WIDTH)
    value_blocks = value_piece.reshape(count, row_count, kv_heads, HEAD_WIDTH)
    starts = row_count * jnp.arange(count, dtype=jnp.int32)

    def advance(inner, item):
        key_block, value_block, block_start = item
        key_pos = positions(span_order, block_start, row_count, sub_rows)
        return (visit(inner, key_block, value_block, key_pos), None)

    carried, unused = lax.scan(advance, carried, (key_blocks, value_blocks, starts))
    maxima, totals, sums = carried

    def column_block(key_block, key_pos):

        def compute():
            scores = (
                jnp.einsum(
                    "qhgd,khd->hgqk", query_mat, key_block, preferred_element_type=jnp.float32
                )
                * score_scale
            )
            allowed = key_pos[None, None, None, :] <= query_pos[None, None, :, None]
            expo = jnp.where(
                allowed, jnp.exp(jnp.where(allowed, scores, NEG) - maxima[..., None]), 0.0
            )
            return jnp.sum(expo / totals[..., None], axis=(1, 2))

        needed = jnp.min(key_pos) <= jnp.max(query_pos)
        return lax.cond(
            needed, compute, lambda: jnp.zeros((kv_heads, key_block.shape[0]), jnp.float32)
        )

    key_piece = lax.all_gather(keys, ("ctx", "rep"), axis=0, tiled=True)
    length = key_piece.shape[0]
    count = length // row_count
    key_blocks = key_piece.reshape(count, row_count, kv_heads, HEAD_WIDTH)
    starts = row_count * jnp.arange(count, dtype=jnp.int32)

    def single_block(item):
        key_block, block_start = item
        return column_block(key_block, positions(span_order, block_start, row_count, sub_rows))

    column_span = lax.map(single_block, (key_blocks, starts))
    column_terms = column_span.transpose(1, 0, 2).reshape(kv_heads, length)
    heavy = (
        lax.psum_scatter(column_terms, ("ctx", "rep"), scatter_dimension=1, tiled=True)
        / group_width
    )
    attended = (
        (sums / totals[..., None])
        .transpose(2, 0, 1, 3)
        .reshape(row_count, kv_heads * group_width * HEAD_WIDTH)
        .astype(jnp.bfloat16)
    )
    return (attended, heavy)


CHIPS = 4
HEADS = 8
ROWS = 256
PAIR = 2 * ROWS
RATE = HEAD_WIDTH ** (-0.5) * math.log2(math.e)
MESH = pl.DeviceIdType.MESH
NT = (((1,), (1,)), ((), ()))
NN = (((1,), (0,)), ((), ()))


def fused_kernel(
    order,
    q_hbm,
    k_hbm,
    v_hbm,
    out_hbm,
    heavy_ref,
    qbuf,
    kbuf,
    vbuf,
    vturn,
    expo,
    top,
    total,
    tops,
    factor,
    sums,
    obuf,
    hacc,
    hsend,
    hrecv,
    local_sem,
    q_send,
    q_recv,
    kv_send,
    kv_recv,
    fwd_send,
    h_sent,
    h_recv,
    o_local,
    o_send,
    o_recv,
):
    group = lax.axis_index("groups")
    z = lax.axis_index("ctx")
    x = lax.axis_index("head")
    c = lax.axis_index("rep")
    other = 1 - c

    def at(zz, cc):
        return (group, zz, x, cc)

    low = 1 - z // 2
    near = low * z + (1 - low) * (CHIPS - 1 - z)

    def chip_of(step):
        end = step
        inner = step + 1 - 3 * (step // 3)
        away = (1 - near) * end + near * inner
        away = away - near * (step // 3)
        return low * away + (1 - low) * (CHIPS - 1 - away)

    wide = HEADS * HEAD_WIDTH
    own_cols = pl.ds(pl.multiple_of(c * wide, wide), wide)
    other_cols = pl.ds(pl.multiple_of(other * wide, wide), wide)
    own_head = pl.ds(pl.multiple_of(c * HEAD_WIDTH, HEAD_WIDTH), HEAD_WIDTH)
    other_head = pl.ds(pl.multiple_of(other * HEAD_WIDTH, HEAD_WIDTH), HEAD_WIDTH)

    local = [
        pltpu.make_async_copy(k_hbm.at[:, own_head], kbuf.at[z, c], local_sem.at[0]),
        pltpu.make_async_copy(q_hbm.at[:, own_cols], qbuf.at[c], local_sem.at[1]),
        pltpu.make_async_copy(v_hbm.at[:, own_head], vbuf.at[z, c], local_sem.at[2]),
    ]
    for copy in local:
        copy.start()

    barrier = pltpu.get_barrier_semaphore()
    pl.semaphore_signal(barrier, inc=1, device_id=at(z, other), device_id_type=MESH)
    for away in range(1, CHIPS):
        for cc in range(2):
            pl.semaphore_signal(
                barrier,
                inc=1,
                device_id=at(lax.rem(z + away, CHIPS), cc),
                device_id_type=MESH,
            )
    pl.semaphore_wait(barrier, 2 * CHIPS - 1)

    def remote(src, dst, send, recv, zz, cc):
        return pltpu.make_async_remote_copy(
            src_ref=src,
            dst_ref=dst,
            send_sem=send,
            recv_sem=recv,
            device_id=at(zz, cc),
            device_id_type=MESH,
        )

    pairs = ((k_hbm, kbuf), (v_hbm, vbuf))

    def sibling_copy(kind):
        src, buf = pairs[kind]
        return remote(
            src.at[:, other_head],
            buf.at[z, c],
            kv_send.at[kind, 4, 0],
            kv_recv.at[kind, z, c],
            z,
            other,
        )

    def chip_copy(kind, slot, zz, cc):
        src, buf = pairs[kind]
        return remote(
            src.at[:, pl.ds(cc * HEAD_WIDTH, HEAD_WIDTH)],
            buf.at[z, c],
            kv_send.at[kind, slot, cc],
            kv_recv.at[kind, z, c],
            zz,
            cc,
        )

    def each_target(kind, act):
        @pl.when(z < CHIPS - 1)
        def _():
            for cc in range(2):
                act(chip_copy(kind, 0, z + 1, cc))

        @pl.when(z > 0)
        def _():
            for cc in range(2):
                act(chip_copy(kind, 1, z - 1, cc))

        @pl.when(z == 0)
        def _():
            for cc in range(2):
                act(chip_copy(kind, 2, z + 2, cc))

        @pl.when(z == CHIPS - 1)
        def _():
            for cc in range(2):
                act(chip_copy(kind, 3, z - 2, cc))

    def forward_copy(kind, step, cc):
        buf = pairs[kind][1]
        zs = chip_of(step)
        return remote(
            buf.at[zs, cc],
            buf.at[zs, cc],
            fwd_send.at[kind, step - 1, cc],
            kv_recv.at[kind, zs, cc],
            (1 - low) * (CHIPS - 1),
            c,
        )

    def wait_block(kind, zz, cc):
        buf = pairs[kind][1]
        remote(
            buf.at[zz, cc],
            buf.at[zz, cc],
            kv_send.at[kind, 4, 1],
            kv_recv.at[kind, zz, cc],
            z,
            other,
        ).wait_recv()

    q_copy = remote(q_hbm.at[:, other_cols], qbuf.at[c], q_send, q_recv, z, other)
    k_side = sibling_copy(0)
    v_side = sibling_copy(1)
    each_target(0, lambda copy: copy.start())
    k_side.start()
    q_copy.start()
    each_target(1, lambda copy: copy.start())
    v_side.start()

    key_row = lax.broadcasted_iota(jnp.int32, (ROWS, ROWS), 0)
    query_lane = lax.broadcasted_iota(jnp.int32, (ROWS, ROWS), 1)

    def score_piece(step, zs, hd, j, first):
        kk = kbuf[zs].reshape(PAIR, HEAD_WIDTH)
        cols = pl.ds(pl.multiple_of(hd * HEAD_WIDTH, HEAD_WIDTH), HEAD_WIDTH)
        scores = lax.dot_general(kk, qbuf[j, :, cols], NT, preferred_element_type=jnp.float32)
        halves, penalties = [], []
        for kb in range(2):
            half = scores[kb * ROWS : (kb + 1) * ROWS]
            if first and kb == j:
                half = jnp.where(key_row <= query_lane, half, NEG)
                penalties.append(jnp.float32(0.0))
            else:
                penalties.append(
                    jnp.where(order[2 * zs + kb] < order[2 * z + j], 0.0, NEG).astype(jnp.float32)
                )
            halves.append(half)
        lanes = pl.ds(j * ROWS, ROWS)
        fresh = jnp.maximum(
            jnp.max(halves[0], axis=0, keepdims=True) + penalties[0],
            jnp.max(halves[1], axis=0, keepdims=True) + penalties[1],
        )
        if not first:
            before = top[hd, :, lanes]
            fresh = jnp.maximum(fresh, before)
        summed = None
        for kb in range(2):
            power = jnp.exp2((halves[kb] - (fresh - penalties[kb])) * RATE)
            expo[step, hd, pl.ds(kb * ROWS, ROWS), lanes] = power.astype(jnp.bfloat16)
            part = jnp.sum(power, axis=0, keepdims=True)
            summed = part if summed is None else summed + part
        if not first:
            summed = summed + total[hd, :, lanes] * jnp.exp2((before - fresh) * RATE)
        top[hd, :, lanes] = fresh
        tops[step, hd, :, lanes] = fresh
        total[hd, :, lanes] = summed

    local[0].wait()
    local[1].wait()
    wait_block(0, z, other)
    q_copy.wait_recv()

    def own_head_scores(hd, carry):
        for j in range(2):
            score_piece(0, z, hd, j, True)
        return carry

    lax.fori_loop(0, HEADS, own_head_scores, 0)

    inner_chip = (z == 1) | (z == 2)

    def score_step(step, carry):
        zs = chip_of(step)
        for cc in range(2):
            wait_block(0, zs, cc)

        @pl.when(inner_chip & (step < 3))
        def _():
            for cc in range(2):
                forward_copy(0, step, cc).start()

        @pl.when(inner_chip & (step == 3))
        def _():
            for cc in range(2):
                wait_block(1, chip_of(1), cc)
            for cc in range(2):
                forward_copy(1, 1, cc).start()

        def head_scores(hd, inner):
            for j in range(2):
                score_piece(step, zs, hd, j, False)
            return inner

        lax.fori_loop(0, HEADS, head_scores, 0)
        return carry

    lax.fori_loop(1, CHIPS, score_step, 0)

    @pl.when(inner_chip)
    def _():
        for cc in range(2):
            wait_block(1, chip_of(2), cc)
        for cc in range(2):
            forward_copy(1, 2, cc).start()

    def scale_step(hd, carry):
        inverse = 1.0 / total[hd]
        for step in range(CHIPS):
            factor[step, hd] = jnp.exp2((tops[step, hd] - top[hd]) * RATE) * inverse
        return carry

    lax.fori_loop(0, HEADS, scale_step, 0)

    def heavy_copy(step, j, zs):
        return remote(
            hsend.at[step, :, pl.ds(j * ROWS, ROWS)],
            hrecv.at[z, c],
            h_sent.at[step, j],
            h_recv.at[z, c],
            zs,
            j,
        )

    def column_step(step, carry):
        share = [factor[step, hd].astype(jnp.bfloat16) for hd in range(HEADS)]

        def tile(t, inner):
            rows = pl.ds(pl.multiple_of(t * 32, 32), 32)
            parts = [expo[step, hd, rows, :] * share[hd] for hd in range(HEADS)]
            while len(parts) > 1:
                parts = [parts[i] + parts[i + 1] for i in range(0, len(parts), 2)]
            hacc[rows, :] = parts[0]
            return inner

        lax.fori_loop(0, PAIR // 32, tile, 0)
        ones = jnp.ones((8, PAIR), jnp.bfloat16)
        hsend[step] = lax.dot_general(ones, hacc[...], NT, preferred_element_type=jnp.float32) * (
            1.0 / HEADS
        )
        return carry

    lax.fori_loop(0, CHIPS, column_step, 0)

    for step in range(1, CHIPS):
        for j in range(2):
            heavy_copy(step, j, chip_of(step)).start()
    for j in range(2):

        @pl.when(c == j)
        def _():
            hrecv[z, c] = hsend[0, :, j * ROWS : (j + 1) * ROWS]

        @pl.when(c != j)
        def _():
            heavy_copy(0, j, z).start()

    local[2].wait()
    wait_block(1, z, other)

    def turn(zs):
        vturn[...] = vbuf[zs].reshape(PAIR, HEAD_WIDTH).T

    def product(step, hd):
        return (
            lax.dot_general(vturn[...], expo[step, hd], NN, preferred_element_type=jnp.float32)
            * factor[step, hd]
        )

    turn(z)

    def own_values(hd, carry):
        sums[hd] = product(0, hd)
        return carry

    lax.fori_loop(0, HEADS, own_values, 0)

    def wait_values(step):
        zs = chip_of(step)
        for cc in range(2):
            wait_block(1, zs, cc)

    def value_step(step, carry):
        @pl.when(jnp.logical_not(inner_chip))
        def _():
            wait_values(step)

        turn(chip_of(step))

        def head_values(hd, inner):
            sums[hd] += product(step, hd)
            return inner

        lax.fori_loop(0, HEADS, head_values, 0)
        return carry

    lax.fori_loop(1, CHIPS - 1, value_step, 0)
    wait_values(CHIPS - 1)
    turn(chip_of(CHIPS - 1))

    def out_cols(hd):
        return pl.ds(pl.multiple_of(c * wide + hd * HEAD_WIDTH, HEAD_WIDTH), HEAD_WIDTH)

    def own_out(hd):
        return pltpu.make_async_copy(obuf.at[c, hd], out_hbm.at[:, out_cols(hd)], o_local.at[hd])

    def other_out(hd):
        return remote(
            obuf.at[other, hd],
            out_hbm.at[:, out_cols(hd)],
            o_send.at[hd],
            o_recv.at[hd],
            z,
            other,
        )

    def last_values(hd, carry):
        done = (sums[hd] + product(CHIPS - 1, hd)).astype(jnp.bfloat16)
        for j in range(2):
            obuf[j, hd] = done[:, j * ROWS : (j + 1) * ROWS].T
        other_out(hd).start()
        own_out(hd).start()
        return carry

    lax.fori_loop(0, HEADS, last_values, 0)

    for zz in range(CHIPS):
        for cc in range(2):

            @pl.when((z != zz) | (c != cc))
            def _():
                remote(
                    hrecv.at[zz, cc],
                    hrecv.at[zz, cc],
                    h_sent.at[0, 0],
                    h_recv.at[zz, cc],
                    z,
                    other,
                ).wait_recv()

    for cc in range(2):
        row = hrecv[0, cc, 0:1, :]
        for zz in range(1, CHIPS):
            row = row + hrecv[zz, cc, 0:1, :]
        heavy_ref[cc : cc + 1, :] = row

    for step in range(1, CHIPS):
        for j in range(2):
            heavy_copy(step, j, chip_of(step)).wait_send()
    for j in range(2):

        @pl.when(c != j)
        def _():
            heavy_copy(0, j, z).wait_send()

    q_copy.wait_send()
    for kind in range(2):
        each_target(kind, lambda copy: copy.wait_send())
    k_side.wait_send()
    v_side.wait_send()

    @pl.when(inner_chip)
    def _():
        for kind in range(2):
            for step in range(1, 3):
                for cc in range(2):
                    forward_copy(kind, step, cc).wait_send()

    def finish(hd, carry):
        own_out(hd).wait()
        other_out(hd).wait()
        return carry

    lax.fori_loop(0, HEADS, finish, 0)


def fused_on_device(queries, keys, values, span_order):
    width = queries.shape[1]
    any_space = pl.BlockSpec(memory_space=pl.ANY)
    dma = pltpu.SemaphoreType.DMA
    return pl.pallas_call(
        fused_kernel,
        out_shape=(
            jax.ShapeDtypeStruct((ROWS, width), jnp.bfloat16),
            jax.ShapeDtypeStruct((2, ROWS), jnp.float32),
        ),
        in_specs=[pl.BlockSpec(memory_space=pltpu.SMEM), any_space, any_space, any_space],
        out_specs=(any_space, pl.BlockSpec(memory_space=pltpu.VMEM)),
        scratch_shapes=[
            pltpu.VMEM((2, ROWS, HEADS * HEAD_WIDTH), jnp.bfloat16),
            pltpu.VMEM((CHIPS, 2, ROWS, HEAD_WIDTH), jnp.bfloat16),
            pltpu.VMEM((CHIPS, 2, ROWS, HEAD_WIDTH), jnp.bfloat16),
            pltpu.VMEM((HEAD_WIDTH, PAIR), jnp.bfloat16),
            pltpu.VMEM((CHIPS, HEADS, PAIR, PAIR), jnp.bfloat16),
            pltpu.VMEM((HEADS, 1, PAIR), jnp.float32),
            pltpu.VMEM((HEADS, 1, PAIR), jnp.float32),
            pltpu.VMEM((CHIPS, HEADS, 1, PAIR), jnp.float32),
            pltpu.VMEM((CHIPS, HEADS, 1, PAIR), jnp.float32),
            pltpu.VMEM((HEADS, HEAD_WIDTH, PAIR), jnp.float32),
            pltpu.VMEM((2, HEADS, ROWS, HEAD_WIDTH), jnp.bfloat16),
            pltpu.VMEM((PAIR, PAIR), jnp.bfloat16),
            pltpu.VMEM((CHIPS, 8, PAIR), jnp.float32),
            pltpu.VMEM((CHIPS, 2, 8, ROWS), jnp.float32),
            dma((3,)),
            dma,
            dma,
            dma((2, 5, 2)),
            dma((2, CHIPS, 2)),
            dma((2, 2, 2)),
            dma((CHIPS, 2)),
            dma((CHIPS, 2)),
            dma((HEADS,)),
            dma((HEADS,)),
            dma((HEADS,)),
        ],
        compiler_params=pltpu.CompilerParams(
            collective_id=0, has_side_effects=True, vmem_limit_bytes=48 * 2**20
        ),
    )(span_order, queries, keys, values)


def solution(mesh):
    placed = (
        P(("groups", "ctx", "rep"), "head"),
        P(("groups", "ctx", "rep"), "head"),
        P(("groups", "ctx", "rep"), "head"),
        P("groups"),
    )
    fits = (
        mesh.shape["ctx"] == CHIPS and mesh.shape["rep"] == 2 and mesh.shape["head"] == 2
    )
    return jax.shard_map(
        fused_on_device if fits else on_device,
        mesh=mesh,
        in_specs=placed,
        out_specs=(P(("groups", "ctx", "rep"), "head"), P(("groups", "head"), ("ctx", "rep"))),
        check_vma=False,
    )
```

```python
import functools
import math

import jax
import jax.numpy as jnp
from jax import lax
from jax.experimental import pallas as pl
from jax.experimental.pallas import tpu as pltpu
from jax.sharding import PartitionSpec as P

HEAD_WIDTH = 128
SPLIT = 1


NEG = -1e30


def positions(order_table, first_row, count, sub_rows):
    row_index = first_row + jnp.arange(count, dtype=jnp.int32)
    return jnp.take(order_table, row_index // sub_rows) * sub_rows + row_index % sub_rows


def absorb(carried, key_block, value_block, key_pos, query_part, pos_part, score_scale):
    maxima, totals, sums = carried
    scores = (
        jnp.einsum("qhgd,khd->hgqk", query_part, key_block, preferred_element_type=jnp.float32)
        * score_scale
    )
    allowed = key_pos[None, None, None, :] <= pos_part[None, None, :, None]
    scores = jnp.where(allowed, scores, NEG)
    fresh = jnp.maximum(maxima, jnp.max(scores, axis=-1))
    expo = jnp.where(allowed, jnp.exp(scores - fresh[..., None]), 0.0)
    factor = jnp.exp(maxima - fresh)
    totals = totals * factor + jnp.sum(expo, axis=-1)
    weights = expo.astype(jnp.bfloat16)
    sums = sums * factor[..., None] + jnp.einsum(
        "hgqk,khd->hgqd", weights, value_block, preferred_element_type=jnp.float32
    )
    return (fresh, totals, sums)


def on_device(queries, keys, values, span_order):
    row_count = queries.shape[0]
    kv_heads = keys.shape[1] // HEAD_WIDTH
    group_width = queries.shape[1] // keys.shape[1]
    sub_rows = row_count // SPLIT
    score_scale = HEAD_WIDTH ** (-0.5)
    device_rank = lax.axis_index(("ctx", "rep"))
    query_pos = positions(span_order, device_rank * row_count, row_count, sub_rows)
    query_mat = queries.reshape(row_count, kv_heads, group_width, HEAD_WIDTH)

    def visit(carried, key_block, value_block, key_pos):
        needed = jnp.min(key_pos) <= jnp.max(query_pos)
        return lax.cond(
            needed,
            lambda inner: absorb(
                inner, key_block, value_block, key_pos, query_mat, query_pos, score_scale
            ),
            lambda inner: inner,
            carried,
        )

    initial = (
        jnp.full((kv_heads, group_width, row_count), NEG, jnp.float32),
        jnp.zeros((kv_heads, group_width, row_count), jnp.float32),
        jnp.zeros((kv_heads, group_width, row_count, HEAD_WIDTH), jnp.float32),
    )
    carried = initial
    key_piece = lax.all_gather(keys, ("ctx", "rep"), axis=0, tiled=True)
    value_piece = lax.all_gather(values, ("ctx", "rep"), axis=0, tiled=True)
    length = key_piece.shape[0]
    count = length // row_count
    key_blocks = key_piece.reshape(count, row_count, kv_heads, HEAD_WIDTH)
    value_blocks = value_piece.reshape(count, row_count, kv_heads, HEAD_WIDTH)
    starts = row_count * jnp.arange(count, dtype=jnp.int32)

    def advance(inner, item):
        key_block, value_block, block_start = item
        key_pos = positions(span_order, block_start, row_count, sub_rows)
        return (visit(inner, key_block, value_block, key_pos), None)

    carried, unused = lax.scan(advance, carried, (key_blocks, value_blocks, starts))
    maxima, totals, sums = carried

    def column_block(key_block, key_pos):

        def compute():
            scores = (
                jnp.einsum(
                    "qhgd,khd->hgqk", query_mat, key_block, preferred_element_type=jnp.float32
                )
                * score_scale
            )
            allowed = key_pos[None, None, None, :] <= query_pos[None, None, :, None]
            expo = jnp.where(
                allowed, jnp.exp(jnp.where(allowed, scores, NEG) - maxima[..., None]), 0.0
            )
            return jnp.sum(expo / totals[..., None], axis=(1, 2))

        needed = jnp.min(key_pos) <= jnp.max(query_pos)
        return lax.cond(
            needed, compute, lambda: jnp.zeros((kv_heads, key_block.shape[0]), jnp.float32)
        )

    key_piece = lax.all_gather(keys, ("ctx", "rep"), axis=0, tiled=True)
    length = key_piece.shape[0]
    count = length // row_count
    key_blocks = key_piece.reshape(count, row_count, kv_heads, HEAD_WIDTH)
    starts = row_count * jnp.arange(count, dtype=jnp.int32)

    def single_block(item):
        key_block, block_start = item
        return column_block(key_block, positions(span_order, block_start, row_count, sub_rows))

    column_span = lax.map(single_block, (key_blocks, starts))
    column_terms = column_span.transpose(1, 0, 2).reshape(kv_heads, length)
    heavy = (
        lax.psum_scatter(column_terms, ("ctx", "rep"), scatter_dimension=1, tiled=True)
        / group_width
    )
    attended = (
        (sums / totals[..., None])
        .transpose(2, 0, 1, 3)
        .reshape(row_count, kv_heads * group_width * HEAD_WIDTH)
        .astype(jnp.bfloat16)
    )
    return (attended, heavy)


CHIPS = 4
HEADS = 8
BATCH = 4
ROWS = 256
PAIR = 2 * ROWS
RATE = HEAD_WIDTH ** (-0.5) * math.log2(math.e)
MESH = pl.DeviceIdType.MESH
NT = (((1,), (1,)), ((), ()))
NN = (((1,), (0,)), ((), ()))


def fused_kernel(
    order,
    q_hbm,
    k_hbm,
    v_hbm,
    out_hbm,
    heavy_ref,
    qbuf,
    kbuf,
    vbuf,
    vturn,
    expo,
    top,
    total,
    tops,
    factor,
    sums,
    obuf,
    hacc,
    hsend,
    hrecv,
    local_sem,
    q_send,
    q_recv,
    kv_send,
    kv_recv,
    fwd_send,
    h_sent,
    h_recv,
    o_local,
    o_send,
    o_recv,
):
    group = lax.axis_index("groups")
    z = lax.axis_index("ctx")
    x = lax.axis_index("head")
    c = lax.axis_index("rep")
    other = 1 - c

    def at(zz, cc):
        return (group, zz, x, cc)

    low = 1 - z // 2
    near = low * z + (1 - low) * (CHIPS - 1 - z)

    def chip_of(step):
        end = step
        inner = step + 1 - 3 * (step // 3)
        away = (1 - near) * end + near * inner
        away = away - near * (step // 3)
        return low * away + (1 - low) * (CHIPS - 1 - away)

    wide = HEADS * HEAD_WIDTH
    own_cols = pl.ds(pl.multiple_of(c * wide, wide), wide)
    other_cols = pl.ds(pl.multiple_of(other * wide, wide), wide)
    own_head = pl.ds(pl.multiple_of(c * HEAD_WIDTH, HEAD_WIDTH), HEAD_WIDTH)
    other_head = pl.ds(pl.multiple_of(other * HEAD_WIDTH, HEAD_WIDTH), HEAD_WIDTH)

    local = [
        pltpu.make_async_copy(k_hbm.at[:, own_head], kbuf.at[z, c], local_sem.at[0]),
        pltpu.make_async_copy(q_hbm.at[:, own_cols], qbuf.at[c], local_sem.at[1]),
        pltpu.make_async_copy(v_hbm.at[:, own_head], vbuf.at[z, c], local_sem.at[2]),
    ]
    for copy in local:
        copy.start()

    barrier = pltpu.get_barrier_semaphore()
    pl.semaphore_signal(barrier, inc=1, device_id=at(z, other), device_id_type=MESH)
    for away in range(1, CHIPS):
        for cc in range(2):
            pl.semaphore_signal(
                barrier,
                inc=1,
                device_id=at(lax.rem(z + away, CHIPS), cc),
                device_id_type=MESH,
            )
    pl.semaphore_wait(barrier, 2 * CHIPS - 1)

    def remote(src, dst, send, recv, zz, cc):
        return pltpu.make_async_remote_copy(
            src_ref=src,
            dst_ref=dst,
            send_sem=send,
            recv_sem=recv,
            device_id=at(zz, cc),
            device_id_type=MESH,
        )

    pairs = ((k_hbm, kbuf), (v_hbm, vbuf))

    def sibling_copy(kind):
        src, buf = pairs[kind]
        return remote(
            src.at[:, other_head],
            buf.at[z, c],
            kv_send.at[kind, 4, 0],
            kv_recv.at[kind, z, c],
            z,
            other,
        )

    def chip_copy(kind, slot, zz, cc):
        src, buf = pairs[kind]
        return remote(
            src.at[:, pl.ds(cc * HEAD_WIDTH, HEAD_WIDTH)],
            buf.at[z, c],
            kv_send.at[kind, slot, cc],
            kv_recv.at[kind, z, c],
            zz,
            cc,
        )

    def each_target(kind, act, outward=True, inward=True):
        ups = (((z == 2), outward), ((z < 2), inward))
        downs = (((z == 1), outward), ((z > 1), inward))
        for conditions, slot, zz in ((ups, 0, z + 1), (downs, 1, z - 1)):
            for condition, wanted in conditions:
                if wanted:

                    @pl.when(condition)
                    def _():
                        for cc in range(2):
                            act(chip_copy(kind, slot, zz, cc))

        if inward:

            @pl.when(z == 0)
            def _():
                for cc in range(2):
                    act(chip_copy(kind, 2, z + 2, cc))

            @pl.when(z == CHIPS - 1)
            def _():
                for cc in range(2):
                    act(chip_copy(kind, 3, z - 2, cc))

    def forward_copy(kind, step, cc):
        buf = pairs[kind][1]
        zs = chip_of(step)
        return remote(
            buf.at[zs, cc],
            buf.at[zs, cc],
            fwd_send.at[kind, step - 1, cc],
            kv_recv.at[kind, zs, cc],
            (1 - low) * (CHIPS - 1),
            c,
        )

    def wait_block(kind, zz, cc):
        buf = pairs[kind][1]
        remote(
            buf.at[zz, cc],
            buf.at[zz, cc],
            kv_send.at[kind, 4, 1],
            kv_recv.at[kind, zz, cc],
            z,
            other,
        ).wait_recv()

    q_copy = remote(q_hbm.at[:, other_cols], qbuf.at[c], q_send, q_recv, z, other)
    k_side = sibling_copy(0)
    v_side = sibling_copy(1)
    each_target(0, lambda copy: copy.start())
    k_side.start()
    q_copy.start()
    v_side.start()
    each_target(1, lambda copy: copy.start(), inward=False)

    key_row = lax.broadcasted_iota(jnp.int32, (ROWS, ROWS), 0)
    query_lane = lax.broadcasted_iota(jnp.int32, (ROWS, ROWS), 1)

    def score_heads(step, zs, heads, first):
        kk = kbuf[zs].reshape(PAIR, HEAD_WIDTH)
        pieces = [(hd, j) for hd in heads for j in range(2)]
        before = []
        if not first:
            for hd, j in pieces:
                lanes = pl.ds(j * ROWS, ROWS)
                before.append((top[hd, :, lanes], total[hd, :, lanes]))
        results = []
        for n, (hd, j) in enumerate(pieces):
            cols = pl.ds(pl.multiple_of(hd * HEAD_WIDTH, HEAD_WIDTH), HEAD_WIDTH)
            scores = lax.dot_general(kk, qbuf[j, :, cols], NT, preferred_element_type=jnp.float32)
            halves, penalties = [], []
            for kb in range(2):
                half = scores[kb * ROWS : (kb + 1) * ROWS]
                if first and kb == j:
                    half = jnp.where(key_row <= query_lane, half, NEG)
                    penalties.append(jnp.float32(0.0))
                else:
                    penalties.append(
                        jnp.where(order[2 * zs + kb] < order[2 * z + j], 0.0, NEG).astype(
                            jnp.float32
                        )
                    )
                halves.append(half)
            fresh = jnp.maximum(
                jnp.max(halves[0], axis=0, keepdims=True) + penalties[0],
                jnp.max(halves[1], axis=0, keepdims=True) + penalties[1],
            )
            if not first:
                fresh = jnp.maximum(fresh, before[n][0])
            summed = None
            for kb in range(2):
                power = jnp.exp2((halves[kb] - (fresh - penalties[kb])) * RATE)
                expo[step, hd, pl.ds(kb * ROWS, ROWS), pl.ds(j * ROWS, ROWS)] = power.astype(
                    jnp.bfloat16
                )
                part = jnp.sum(power, axis=0, keepdims=True)
                summed = part if summed is None else summed + part
            if not first:
                old_top, old_total = before[n]
                summed = summed + old_total * jnp.exp2((old_top - fresh) * RATE)
            results.append((hd, j, fresh, summed))
        for hd, j, fresh, summed in results:
            lanes = pl.ds(j * ROWS, ROWS)
            top[hd, :, lanes] = fresh
            tops[step, hd, :, lanes] = fresh
            total[hd, :, lanes] = summed

    inner_chip = (z == 1) | (z == 2)

    def pass_on(kind, step):
        for cc in range(2):
            wait_block(kind, chip_of(step), cc)
        for cc in range(2):
            forward_copy(kind, step, cc).start()

    @pl.when(inner_chip)
    def _():
        pass_on(0, 1)
        each_target(1, lambda copy: copy.start(), outward=False)

    local[0].wait()
    local[1].wait()
    wait_block(0, z, other)
    q_copy.wait_recv()

    def own_head_scores(t, carry):
        score_heads(0, z, [t * BATCH + b for b in range(BATCH)], True)
        return carry

    lax.fori_loop(0, HEADS // BATCH, own_head_scores, 0)

    @pl.when(jnp.logical_not(inner_chip))
    def _():
        each_target(1, lambda copy: copy.start(), outward=False)

    def wait_keys(zs):
        for cc in range(2):
            wait_block(0, zs, cc)

    def score_step(step, carry):
        zs = chip_of(step)

        @pl.when(jnp.logical_not(inner_chip) | (step == 3))
        def _():
            wait_keys(zs)

        for early, (kind, of) in enumerate(((0, 2), (1, 1), (1, 2))):

            @pl.when(inner_chip & (step == early + 1))
            def _():
                pass_on(kind, of)

        def head_scores(t, inner):
            score_heads(step, zs, [t * BATCH + b for b in range(BATCH)], False)
            return inner

        lax.fori_loop(0, HEADS // BATCH, head_scores, 0)
        return carry

    lax.fori_loop(1, CHIPS, score_step, 0)

    def scale_step(hd, carry):
        inverse = 1.0 / total[hd]
        for step in range(CHIPS):
            factor[step, hd] = jnp.exp2((tops[step, hd] - top[hd]) * RATE) * inverse
        return carry

    lax.fori_loop(0, HEADS, scale_step, 0, unroll=4)

    def heavy_copy(step, j, zs):
        return remote(
            hsend.at[step, :, pl.ds(j * ROWS, ROWS)],
            hrecv.at[z, c],
            h_sent.at[step, j],
            h_recv.at[z, c],
            zs,
            j,
        )

    def column_step(step, carry):
        share = [factor[step, hd].astype(jnp.bfloat16) for hd in range(HEADS)]

        def tile(t, inner):
            rows = pl.ds(pl.multiple_of(t * 32, 32), 32)
            parts = [expo[step, hd, rows, :] * share[hd] for hd in range(HEADS)]
            while len(parts) > 1:
                parts = [parts[i] + parts[i + 1] for i in range(0, len(parts), 2)]
            hacc[rows, :] = parts[0]
            return inner

        lax.fori_loop(0, PAIR // 32, tile, 0, unroll=4)
        ones = jnp.ones((8, PAIR), jnp.bfloat16)
        hsend[step] = lax.dot_general(ones, hacc[...], NT, preferred_element_type=jnp.float32)
        return carry

    lax.fori_loop(0, CHIPS, column_step, 0)

    for step in range(1, CHIPS):
        for j in range(2):
            heavy_copy(step, j, chip_of(step)).start()
    for j in range(2):

        @pl.when(c == j)
        def _():
            hrecv[z, c] = hsend[0, :, j * ROWS : (j + 1) * ROWS]

        @pl.when(c != j)
        def _():
            heavy_copy(0, j, z).start()

    local[2].wait()
    wait_block(1, z, other)

    def turn(zs):
        vturn[...] = vbuf[zs].reshape(PAIR, HEAD_WIDTH).T

    def product(step, hd):
        return (
            lax.dot_general(vturn[...], expo[step, hd], NN, preferred_element_type=jnp.float32)
            * factor[step, hd]
        )

    turn(z)

    def own_values(hd, carry):
        sums[hd] = product(0, hd)
        return carry

    lax.fori_loop(0, HEADS, own_values, 0, unroll=4)

    def wait_values(step):
        zs = chip_of(step)
        for cc in range(2):
            wait_block(1, zs, cc)

    def value_step(step, carry):
        @pl.when(jnp.logical_not(inner_chip))
        def _():
            wait_values(step)

        turn(chip_of(step))

        def head_values(hd, inner):
            sums[hd] += product(step, hd)
            return inner

        lax.fori_loop(0, HEADS, head_values, 0, unroll=4)
        return carry

    lax.fori_loop(1, CHIPS - 1, value_step, 0)
    wait_values(CHIPS - 1)
    turn(chip_of(CHIPS - 1))

    def out_cols(hd):
        return pl.ds(pl.multiple_of(c * wide + hd * HEAD_WIDTH, HEAD_WIDTH), HEAD_WIDTH)

    def own_out(hd):
        return pltpu.make_async_copy(obuf.at[c, hd], out_hbm.at[:, out_cols(hd)], o_local.at[hd])

    def other_out(hd):
        return remote(
            obuf.at[other, hd],
            out_hbm.at[:, out_cols(hd)],
            o_send.at[hd],
            o_recv.at[hd],
            z,
            other,
        )

    def last_values(hd, carry):
        done = (sums[hd] + product(CHIPS - 1, hd)).astype(jnp.bfloat16)
        for j in range(2):
            obuf[j, hd] = done[:, j * ROWS : (j + 1) * ROWS].T
        other_out(hd).start()
        own_out(hd).start()
        return carry

    lax.fori_loop(0, HEADS, last_values, 0, unroll=2)

    for zz in range(CHIPS):
        for cc in range(2):

            @pl.when((z != zz) | (c != cc))
            def _():
                remote(
                    hrecv.at[zz, cc],
                    hrecv.at[zz, cc],
                    h_sent.at[0, 0],
                    h_recv.at[zz, cc],
                    z,
                    other,
                ).wait_recv()

    for cc in range(2):
        row = hrecv[0, cc]
        for zz in range(1, CHIPS):
            row = row + hrecv[zz, cc]
        heavy_ref[cc] = row

    for step in range(1, CHIPS):
        for j in range(2):
            heavy_copy(step, j, chip_of(step)).wait_send()
    for j in range(2):

        @pl.when(c != j)
        def _():
            heavy_copy(0, j, z).wait_send()

    q_copy.wait_send()
    for kind in range(2):
        each_target(kind, lambda copy: copy.wait_send())
    k_side.wait_send()
    v_side.wait_send()

    @pl.when(inner_chip)
    def _():
        for kind in range(2):
            for step in range(1, 3):
                for cc in range(2):
                    forward_copy(kind, step, cc).wait_send()

    def finish(hd, carry):
        own_out(hd).wait()
        other_out(hd).wait()
        return carry

    lax.fori_loop(0, HEADS, finish, 0)


def fused_on_device(queries, keys, values, span_order):
    width = queries.shape[1]
    any_space = pl.BlockSpec(memory_space=pltpu.HBM)
    dma = pltpu.SemaphoreType.DMA
    attended, heavy = pl.pallas_call(
        fused_kernel,
        out_shape=(
            jax.ShapeDtypeStruct((ROWS, width), jnp.bfloat16),
            jax.ShapeDtypeStruct((2, 8, ROWS), jnp.float32),
        ),
        in_specs=[pl.BlockSpec(memory_space=pltpu.SMEM), any_space, any_space, any_space],
        out_specs=(any_space, pl.BlockSpec(memory_space=pltpu.VMEM)),
        scratch_shapes=[
            pltpu.VMEM((2, ROWS, HEADS * HEAD_WIDTH), jnp.bfloat16),
            pltpu.VMEM((CHIPS, 2, ROWS, HEAD_WIDTH), jnp.bfloat16),
            pltpu.VMEM((CHIPS, 2, ROWS, HEAD_WIDTH), jnp.bfloat16),
            pltpu.VMEM((HEAD_WIDTH, PAIR), jnp.bfloat16),
            pltpu.VMEM((CHIPS, HEADS, PAIR, PAIR), jnp.bfloat16),
            pltpu.VMEM((HEADS, 1, PAIR), jnp.float32),
            pltpu.VMEM((HEADS, 1, PAIR), jnp.float32),
            pltpu.VMEM((CHIPS, HEADS, 1, PAIR), jnp.float32),
            pltpu.VMEM((CHIPS, HEADS, 1, PAIR), jnp.float32),
            pltpu.VMEM((HEADS, HEAD_WIDTH, PAIR), jnp.float32),
            pltpu.VMEM((2, HEADS, ROWS, HEAD_WIDTH), jnp.bfloat16),
            pltpu.VMEM((PAIR, PAIR), jnp.bfloat16),
            pltpu.VMEM((CHIPS, 8, PAIR), jnp.float32),
            pltpu.VMEM((CHIPS, 2, 8, ROWS), jnp.float32),
            dma((3,)),
            dma,
            dma,
            dma((2, 5, 2)),
            dma((2, CHIPS, 2)),
            dma((2, 2, 2)),
            dma((CHIPS, 2)),
            dma((CHIPS, 2)),
            dma((HEADS,)),
            dma((HEADS,)),
            dma((HEADS,)),
        ],
        compiler_params=pltpu.CompilerParams(
            collective_id=0, has_side_effects=True, vmem_limit_bytes=63 * 2**20
        ),
    )(span_order, queries, keys, values)
    return attended, heavy[:, 0, :] / HEADS


def solution(mesh):
    placed = (
        P(("groups", "ctx", "rep"), "head"),
        P(("groups", "ctx", "rep"), "head"),
        P(("groups", "ctx", "rep"), "head"),
        P("groups"),
    )
    fits = (
        mesh.shape["ctx"] == CHIPS and mesh.shape["rep"] == 2 and mesh.shape["head"] == 2
    )
    return jax.shard_map(
        fused_on_device if fits else on_device,
        mesh=mesh,
        in_specs=placed,
        out_specs=(P(("groups", "ctx", "rep"), "head"), P(("groups", "head"), ("ctx", "rep"))),
        check_vma=False,
    )
```

```python
import functools
import math

import jax
import jax.numpy as jnp
from jax import lax
from jax.experimental import pallas as pl
from jax.experimental.pallas import tpu as pltpu
from jax.sharding import PartitionSpec as P

HEAD_WIDTH = 128
SPLIT = 1


NEG = -1e30


def positions(order_table, first_row, count, sub_rows):
    row_index = first_row + jnp.arange(count, dtype=jnp.int32)
    return jnp.take(order_table, row_index // sub_rows) * sub_rows + row_index % sub_rows


def absorb(carried, key_block, value_block, key_pos, query_part, pos_part, score_scale):
    maxima, totals, sums = carried
    scores = (
        jnp.einsum("qhgd,khd->hgqk", query_part, key_block, preferred_element_type=jnp.float32)
        * score_scale
    )
    allowed = key_pos[None, None, None, :] <= pos_part[None, None, :, None]
    scores = jnp.where(allowed, scores, NEG)
    fresh = jnp.maximum(maxima, jnp.max(scores, axis=-1))
    expo = jnp.where(allowed, jnp.exp(scores - fresh[..., None]), 0.0)
    factor = jnp.exp(maxima - fresh)
    totals = totals * factor + jnp.sum(expo, axis=-1)
    weights = expo.astype(jnp.bfloat16)
    sums = sums * factor[..., None] + jnp.einsum(
        "hgqk,khd->hgqd", weights, value_block, preferred_element_type=jnp.float32
    )
    return (fresh, totals, sums)


def on_device(queries, keys, values, span_order):
    row_count = queries.shape[0]
    kv_heads = keys.shape[1] // HEAD_WIDTH
    group_width = queries.shape[1] // keys.shape[1]
    sub_rows = row_count // SPLIT
    score_scale = HEAD_WIDTH ** (-0.5)
    device_rank = lax.axis_index(("ctx", "rep"))
    query_pos = positions(span_order, device_rank * row_count, row_count, sub_rows)
    query_mat = queries.reshape(row_count, kv_heads, group_width, HEAD_WIDTH)

    def visit(carried, key_block, value_block, key_pos):
        needed = jnp.min(key_pos) <= jnp.max(query_pos)
        return lax.cond(
            needed,
            lambda inner: absorb(
                inner, key_block, value_block, key_pos, query_mat, query_pos, score_scale
            ),
            lambda inner: inner,
            carried,
        )

    initial = (
        jnp.full((kv_heads, group_width, row_count), NEG, jnp.float32),
        jnp.zeros((kv_heads, group_width, row_count), jnp.float32),
        jnp.zeros((kv_heads, group_width, row_count, HEAD_WIDTH), jnp.float32),
    )
    carried = initial
    key_piece = lax.all_gather(keys, ("ctx", "rep"), axis=0, tiled=True)
    value_piece = lax.all_gather(values, ("ctx", "rep"), axis=0, tiled=True)
    length = key_piece.shape[0]
    count = length // row_count
    key_blocks = key_piece.reshape(count, row_count, kv_heads, HEAD_WIDTH)
    value_blocks = value_piece.reshape(count, row_count, kv_heads, HEAD_WIDTH)
    starts = row_count * jnp.arange(count, dtype=jnp.int32)

    def advance(inner, item):
        key_block, value_block, block_start = item
        key_pos = positions(span_order, block_start, row_count, sub_rows)
        return (visit(inner, key_block, value_block, key_pos), None)

    carried, unused = lax.scan(advance, carried, (key_blocks, value_blocks, starts))
    maxima, totals, sums = carried

    def column_block(key_block, key_pos):

        def compute():
            scores = (
                jnp.einsum(
                    "qhgd,khd->hgqk", query_mat, key_block, preferred_element_type=jnp.float32
                )
                * score_scale
            )
            allowed = key_pos[None, None, None, :] <= query_pos[None, None, :, None]
            expo = jnp.where(
                allowed, jnp.exp(jnp.where(allowed, scores, NEG) - maxima[..., None]), 0.0
            )
            return jnp.sum(expo / totals[..., None], axis=(1, 2))

        needed = jnp.min(key_pos) <= jnp.max(query_pos)
        return lax.cond(
            needed, compute, lambda: jnp.zeros((kv_heads, key_block.shape[0]), jnp.float32)
        )

    key_piece = lax.all_gather(keys, ("ctx", "rep"), axis=0, tiled=True)
    length = key_piece.shape[0]
    count = length // row_count
    key_blocks = key_piece.reshape(count, row_count, kv_heads, HEAD_WIDTH)
    starts = row_count * jnp.arange(count, dtype=jnp.int32)

    def single_block(item):
        key_block, block_start = item
        return column_block(key_block, positions(span_order, block_start, row_count, sub_rows))

    column_span = lax.map(single_block, (key_blocks, starts))
    column_terms = column_span.transpose(1, 0, 2).reshape(kv_heads, length)
    heavy = (
        lax.psum_scatter(column_terms, ("ctx", "rep"), scatter_dimension=1, tiled=True)
        / group_width
    )
    attended = (
        (sums / totals[..., None])
        .transpose(2, 0, 1, 3)
        .reshape(row_count, kv_heads * group_width * HEAD_WIDTH)
        .astype(jnp.bfloat16)
    )
    return (attended, heavy)


CHIPS = 4
HEADS = 8
BATCH = 4
ROWS = 256
PAIR = 2 * ROWS
RATE = HEAD_WIDTH ** (-0.5) * math.log2(math.e)
MESH = pl.DeviceIdType.MESH
NT = (((1,), (1,)), ((), ()))
NN = (((1,), (0,)), ((), ()))


def fused_kernel(
    order,
    q_hbm,
    k_hbm,
    v_hbm,
    out_hbm,
    heavy_ref,
    qbuf,
    kbuf,
    vbuf,
    vturn,
    expo,
    top,
    total,
    tops,
    factor,
    sums,
    obuf,
    hacc,
    hsend,
    hrecv,
    local_sem,
    q_send,
    q_recv,
    kv_send,
    kv_recv,
    fwd_send,
    h_sent,
    h_recv,
    o_local,
    o_send,
    o_recv,
):
    group = lax.axis_index("groups")
    z = lax.axis_index("ctx")
    x = lax.axis_index("head")
    c = lax.axis_index("rep")
    other = 1 - c

    def at(zz, cc):
        return (group, zz, x, cc)

    low = 1 - z // 2
    near = low * z + (1 - low) * (CHIPS - 1 - z)

    def chip_of(step):
        end = step
        inner = step + 1 - 3 * (step // 3)
        away = (1 - near) * end + near * inner
        away = away - near * (step // 3)
        return low * away + (1 - low) * (CHIPS - 1 - away)

    wide = HEADS * HEAD_WIDTH
    own_cols = pl.ds(pl.multiple_of(c * wide, wide), wide)
    other_cols = pl.ds(pl.multiple_of(other * wide, wide), wide)
    own_head = pl.ds(pl.multiple_of(c * HEAD_WIDTH, HEAD_WIDTH), HEAD_WIDTH)
    other_head = pl.ds(pl.multiple_of(other * HEAD_WIDTH, HEAD_WIDTH), HEAD_WIDTH)

    local = [
        pltpu.make_async_copy(k_hbm.at[:, own_head], kbuf.at[z, c], local_sem.at[0]),
        pltpu.make_async_copy(q_hbm.at[:, own_cols], qbuf.at[c], local_sem.at[1]),
        pltpu.make_async_copy(v_hbm.at[:, own_head], vbuf.at[z, c], local_sem.at[2]),
    ]
    for copy in local:
        copy.start()

    barrier = pltpu.get_barrier_semaphore()
    pl.semaphore_signal(barrier, inc=1, device_id=at(z, other), device_id_type=MESH)
    for away in range(1, CHIPS):
        for cc in range(2):
            pl.semaphore_signal(
                barrier,
                inc=1,
                device_id=at(lax.rem(z + away, CHIPS), cc),
                device_id_type=MESH,
            )
    pl.semaphore_wait(barrier, 2 * CHIPS - 1)

    def remote(src, dst, send, recv, zz, cc):
        return pltpu.make_async_remote_copy(
            src_ref=src,
            dst_ref=dst,
            send_sem=send,
            recv_sem=recv,
            device_id=at(zz, cc),
            device_id_type=MESH,
        )

    pairs = ((k_hbm, kbuf), (v_hbm, vbuf))

    def sibling_copy(kind):
        src, buf = pairs[kind]
        return remote(
            src.at[:, other_head],
            buf.at[z, c],
            kv_send.at[kind, 4, 0],
            kv_recv.at[kind, z, c],
            z,
            other,
        )

    def chip_copy(kind, slot, zz, cc):
        src, buf = pairs[kind]
        return remote(
            src.at[:, pl.ds(cc * HEAD_WIDTH, HEAD_WIDTH)],
            buf.at[z, c],
            kv_send.at[kind, slot, cc],
            kv_recv.at[kind, z, c],
            zz,
            cc,
        )

    def each_target(kind, act, outward=True, inward=True):
        ups = (((z == 2), outward), ((z < 2), inward))
        downs = (((z == 1), outward), ((z > 1), inward))
        for conditions, slot, zz in ((ups, 0, z + 1), (downs, 1, z - 1)):
            for condition, wanted in conditions:
                if wanted:

                    @pl.when(condition)
                    def _():
                        for cc in range(2):
                            act(chip_copy(kind, slot, zz, cc))

        if inward:

            @pl.when(z == 0)
            def _():
                for cc in range(2):
                    act(chip_copy(kind, 2, z + 2, cc))

            @pl.when(z == CHIPS - 1)
            def _():
                for cc in range(2):
                    act(chip_copy(kind, 3, z - 2, cc))

    def forward_copy(kind, step, cc):
        buf = pairs[kind][1]
        zs = chip_of(step)
        return remote(
            buf.at[zs, cc],
            buf.at[zs, cc],
            fwd_send.at[kind, step - 1, cc],
            kv_recv.at[kind, zs, cc],
            (1 - low) * (CHIPS - 1),
            c,
        )

    def wait_block(kind, zz, cc):
        buf = pairs[kind][1]
        remote(
            buf.at[zz, cc],
            buf.at[zz, cc],
            kv_send.at[kind, 4, 1],
            kv_recv.at[kind, zz, cc],
            z,
            other,
        ).wait_recv()

    q_copy = remote(q_hbm.at[:, other_cols], qbuf.at[c], q_send, q_recv, z, other)
    k_side = sibling_copy(0)
    v_side = sibling_copy(1)
    each_target(0, lambda copy: copy.start())
    k_side.start()
    q_copy.start()
    v_side.start()
    each_target(1, lambda copy: copy.start(), inward=False)

    key_row = lax.broadcasted_iota(jnp.int32, (ROWS, ROWS), 0)
    query_lane = lax.broadcasted_iota(jnp.int32, (ROWS, ROWS), 1)

    def score_heads(step, zs, heads, first):
        kk = kbuf[zs].reshape(PAIR, HEAD_WIDTH)
        pieces = [(hd, j) for hd in heads for j in range(2)]
        before = []
        if not first:
            for hd, j in pieces:
                lanes = pl.ds(j * ROWS, ROWS)
                before.append((top[hd, :, lanes], total[hd, :, lanes]))
        results = []
        for n, (hd, j) in enumerate(pieces):
            cols = pl.ds(pl.multiple_of(hd * HEAD_WIDTH, HEAD_WIDTH), HEAD_WIDTH)
            scores = lax.dot_general(kk, qbuf[j, :, cols], NT, preferred_element_type=jnp.float32)
            halves, penalties = [], []
            for kb in range(2):
                half = scores[kb * ROWS : (kb + 1) * ROWS]
                if first and kb == j:
                    half = jnp.where(key_row <= query_lane, half, NEG)
                    penalties.append(jnp.float32(0.0))
                else:
                    penalties.append(
                        jnp.where(order[2 * zs + kb] < order[2 * z + j], 0.0, NEG).astype(
                            jnp.float32
                        )
                    )
                halves.append(half)
            fresh = jnp.maximum(
                jnp.max(halves[0], axis=0, keepdims=True) + penalties[0],
                jnp.max(halves[1], axis=0, keepdims=True) + penalties[1],
            )
            if not first:
                fresh = jnp.maximum(fresh, before[n][0])
            summed = None
            for kb in range(2):
                power = jnp.exp2((halves[kb] - (fresh - penalties[kb])) * RATE)
                expo[step, hd, pl.ds(kb * ROWS, ROWS), pl.ds(j * ROWS, ROWS)] = power.astype(
                    jnp.bfloat16
                )
                part = jnp.sum(power, axis=0, keepdims=True)
                summed = part if summed is None else summed + part
            if not first:
                old_top, old_total = before[n]
                summed = summed + old_total * jnp.exp2((old_top - fresh) * RATE)
            results.append((hd, j, fresh, summed))
        for hd, j, fresh, summed in results:
            lanes = pl.ds(j * ROWS, ROWS)
            top[hd, :, lanes] = fresh
            tops[step, hd, :, lanes] = fresh
            total[hd, :, lanes] = summed

    inner_chip = (z == 1) | (z == 2)

    def pass_on(kind, step):
        for cc in range(2):
            wait_block(kind, chip_of(step), cc)
        for cc in range(2):
            forward_copy(kind, step, cc).start()

    local[0].wait()
    local[1].wait()
    wait_block(0, z, other)
    q_copy.wait_recv()

    def own_head_scores(t, carry):
        score_heads(0, z, [t * BATCH + b for b in range(BATCH)], True)
        return carry

    lax.fori_loop(0, 1, own_head_scores, 0)
    @pl.when(inner_chip)
    def _():
        pass_on(0, 1)
        each_target(1, lambda copy: copy.start(), outward=False)

    lax.fori_loop(1, HEADS // BATCH, own_head_scores, 0)

    @pl.when(jnp.logical_not(inner_chip))
    def _():
        each_target(1, lambda copy: copy.start(), outward=False)

    def wait_keys(zs):
        for cc in range(2):
            wait_block(0, zs, cc)

    def score_step(step, carry):
        zs = chip_of(step)

        @pl.when(jnp.logical_not(inner_chip) | (step == 3))
        def _():
            wait_keys(zs)

        for early, (kind, of) in enumerate(((0, 2), (1, 1), (1, 2))):

            @pl.when(inner_chip & (step == early + 1))
            def _():
                pass_on(kind, of)

        def head_scores(t, inner):
            score_heads(step, zs, [t * BATCH + b for b in range(BATCH)], False)
            return inner

        lax.fori_loop(0, HEADS // BATCH, head_scores, 0)
        return carry

    lax.fori_loop(1, CHIPS, score_step, 0)

    def scale_step(hd, carry):
        inverse = 1.0 / total[hd]
        for step in range(CHIPS):
            factor[step, hd] = jnp.exp2((tops[step, hd] - top[hd]) * RATE) * inverse
        return carry

    lax.fori_loop(0, HEADS, scale_step, 0, unroll=8)

    def heavy_copy(step, j, zs):
        return remote(
            hsend.at[step, :, pl.ds(j * ROWS, ROWS)],
            hrecv.at[z, c],
            h_sent.at[step, j],
            h_recv.at[z, c],
            zs,
            j,
        )

    def column_step(step, carry):
        share = [factor[step, hd].astype(jnp.bfloat16) for hd in range(HEADS)]

        def tile(t, inner):
            rows = pl.ds(pl.multiple_of(t * 32, 32), 32)
            parts = [expo[step, hd, rows, :] * share[hd] for hd in range(HEADS)]
            while len(parts) > 1:
                parts = [parts[i] + parts[i + 1] for i in range(0, len(parts), 2)]
            hacc[rows, :] = parts[0]
            return inner

        lax.fori_loop(0, PAIR // 32, tile, 0, unroll=8)
        ones = jnp.ones((8, PAIR), jnp.bfloat16)
        hsend[step] = lax.dot_general(ones, hacc[...], NT, preferred_element_type=jnp.float32)
        return carry

    lax.fori_loop(0, CHIPS, column_step, 0)

    for step in range(1, CHIPS):
        for j in range(2):
            heavy_copy(step, j, chip_of(step)).start()
    for j in range(2):

        @pl.when(c == j)
        def _():
            hrecv[z, c] = hsend[0, :, j * ROWS : (j + 1) * ROWS]

        @pl.when(c != j)
        def _():
            heavy_copy(0, j, z).start()

    local[2].wait()
    wait_block(1, z, other)

    def turn(zs):
        vturn[...] = vbuf[zs].reshape(PAIR, HEAD_WIDTH).T

    def product(step, hd):
        return (
            lax.dot_general(vturn[...], expo[step, hd], NN, preferred_element_type=jnp.float32)
            * factor[step, hd]
        )

    turn(z)

    def own_values(hd, carry):
        sums[hd] = product(0, hd)
        return carry

    lax.fori_loop(0, HEADS, own_values, 0, unroll=8)

    def wait_values(step):
        zs = chip_of(step)
        for cc in range(2):
            wait_block(1, zs, cc)

    def value_step(step, carry):
        @pl.when(jnp.logical_not(inner_chip))
        def _():
            wait_values(step)

        turn(chip_of(step))

        def head_values(hd, inner):
            sums[hd] += product(step, hd)
            return inner

        lax.fori_loop(0, HEADS, head_values, 0, unroll=8)
        return carry

    lax.fori_loop(1, CHIPS - 1, value_step, 0)
    wait_values(CHIPS - 1)
    turn(chip_of(CHIPS - 1))

    def out_cols(hd):
        return pl.ds(pl.multiple_of(c * wide + hd * HEAD_WIDTH, HEAD_WIDTH), HEAD_WIDTH)

    def own_out(hd):
        return pltpu.make_async_copy(obuf.at[c, hd], out_hbm.at[:, out_cols(hd)], o_local.at[hd])

    def other_out(hd):
        return remote(
            obuf.at[other, hd],
            out_hbm.at[:, out_cols(hd)],
            o_send.at[hd],
            o_recv.at[hd],
            z,
            other,
        )

    def last_values(hd, carry):
        done = (sums[hd] + product(CHIPS - 1, hd)).astype(jnp.bfloat16)
        for j in range(2):
            obuf[j, hd] = done[:, j * ROWS : (j + 1) * ROWS].T
        other_out(hd).start()
        own_out(hd).start()
        return carry

    lax.fori_loop(0, HEADS, last_values, 0, unroll=2)

    for zz in range(CHIPS):
        for cc in range(2):

            @pl.when((z != zz) | (c != cc))
            def _():
                remote(
                    hrecv.at[zz, cc],
                    hrecv.at[zz, cc],
                    h_sent.at[0, 0],
                    h_recv.at[zz, cc],
                    z,
                    other,
                ).wait_recv()

    for cc in range(2):
        row = hrecv[0, cc, 0:1, :]
        for zz in range(1, CHIPS):
            row = row + hrecv[zz, cc, 0:1, :]
        heavy_ref[cc : cc + 1, :] = row / HEADS

    for step in range(1, CHIPS):
        for j in range(2):
            heavy_copy(step, j, chip_of(step)).wait_send()
    for j in range(2):

        @pl.when(c != j)
        def _():
            heavy_copy(0, j, z).wait_send()

    q_copy.wait_send()
    for kind in range(2):
        each_target(kind, lambda copy: copy.wait_send())
    k_side.wait_send()
    v_side.wait_send()

    @pl.when(inner_chip)
    def _():
        for kind in range(2):
            for step in range(1, 3):
                for cc in range(2):
                    forward_copy(kind, step, cc).wait_send()

    def finish(hd, carry):
        own_out(hd).wait()
        other_out(hd).wait()
        return carry

    lax.fori_loop(0, HEADS, finish, 0)


def fused_on_device(queries, keys, values, span_order):
    width = queries.shape[1]
    any_space = pl.BlockSpec(memory_space=pltpu.HBM)
    dma = pltpu.SemaphoreType.DMA
    attended, heavy = pl.pallas_call(
        fused_kernel,
        out_shape=(
            jax.ShapeDtypeStruct((ROWS, width), jnp.bfloat16),
            jax.ShapeDtypeStruct((2, ROWS), jnp.float32),
        ),
        in_specs=[pl.BlockSpec(memory_space=pltpu.SMEM), any_space, any_space, any_space],
        out_specs=(any_space, pl.BlockSpec(memory_space=pltpu.VMEM)),
        scratch_shapes=[
            pltpu.VMEM((2, ROWS, HEADS * HEAD_WIDTH), jnp.bfloat16),
            pltpu.VMEM((CHIPS, 2, ROWS, HEAD_WIDTH), jnp.bfloat16),
            pltpu.VMEM((CHIPS, 2, ROWS, HEAD_WIDTH), jnp.bfloat16),
            pltpu.VMEM((HEAD_WIDTH, PAIR), jnp.bfloat16),
            pltpu.VMEM((CHIPS, HEADS, PAIR, PAIR), jnp.bfloat16),
            pltpu.VMEM((HEADS, 1, PAIR), jnp.float32),
            pltpu.VMEM((HEADS, 1, PAIR), jnp.float32),
            pltpu.VMEM((CHIPS, HEADS, 1, PAIR), jnp.float32),
            pltpu.VMEM((CHIPS, HEADS, 1, PAIR), jnp.float32),
            pltpu.VMEM((HEADS, HEAD_WIDTH, PAIR), jnp.float32),
            pltpu.VMEM((2, HEADS, ROWS, HEAD_WIDTH), jnp.bfloat16),
            pltpu.VMEM((PAIR, PAIR), jnp.bfloat16),
            pltpu.VMEM((CHIPS, 8, PAIR), jnp.float32),
            pltpu.VMEM((CHIPS, 2, 8, ROWS), jnp.float32),
            dma((3,)),
            dma,
            dma,
            dma((2, 5, 2)),
            dma((2, CHIPS, 2)),
            dma((2, 2, 2)),
            dma((CHIPS, 2)),
            dma((CHIPS, 2)),
            dma((HEADS,)),
            dma((HEADS,)),
            dma((HEADS,)),
        ],
        compiler_params=pltpu.CompilerParams(
            collective_id=0, has_side_effects=True, vmem_limit_bytes=63 * 2**20
        ),
    )(span_order, queries, keys, values)
    return attended, heavy


def solution(mesh):
    placed = (
        P(("groups", "ctx", "rep"), "head"),
        P(("groups", "ctx", "rep"), "head"),
        P(("groups", "ctx", "rep"), "head"),
        P("groups"),
    )
    fits = (
        mesh.shape["ctx"] == CHIPS and mesh.shape["rep"] == 2 and mesh.shape["head"] == 2
    )
    return jax.shard_map(
        fused_on_device if fits else on_device,
        mesh=mesh,
        in_specs=placed,
        out_specs=(P(("groups", "ctx", "rep"), "head"), P(("groups", "head"), ("ctx", "rep"))),
        check_vma=False,
    )
```
